32 devices in a mesh: tok: 8 (over y, x, core), exp: 4 (over z).
Axes of the slice: x: 2, y: 2, z: 4, core: 2. Of those that a mesh axis runs over, the one named last changes fastest.
Arguments:
- tokens: bfloat16 [128, 6144], P('tok', 'exp'), may hold values from -6 to 6
- route_ids: int32 [128, 2], P('tok'), may hold values from 0 to 3, all different within a row; in each aligned block of 16 rows (0 to 15, 16 to 31, ...) at most 12 rows name the same one
- gate_codes: int32 [128, 2], P('tok'), may hold values from 1 to 255
- merge_labels: int32 [4], replicated, may hold values from 0 to 1, as said below
- freq_counts: int32 [4], replicated, may hold values from 1024 to 4096
- w_gate: bfloat16 [32768, 6144], P(('tok', 'exp')), may hold values from -0.078125 to 0.078125
- w_up: bfloat16 [32768, 6144], P(('tok', 'exp')), may hold values from -0.078125 to 0.078125
- w_down: bfloat16 [32768, 6144], P('tok', 'exp'), may hold values from -0.0625 to 0.0625
Outputs:
- initial_out: bfloat16 [128, 6144], P('tok', 'exp')
- merged_out: bfloat16 [128, 6144], P('tok', 'exp')
The draws below stay inside these ranges and needn't reach their ends.
Inputs may be any that keep to these rules, and one draw needn't show every extreme that they name: `route_ids`: the 2 ids of a row differ. Among the 16 rows of one token shard no expert is named more than 12 times, a bound that some block reaches. `merge_labels`: experts with equal labels form one merge group; every group has exactly two experts.
All inputs are finite; a program needn't handle non-finite values.
Results may differ from the reference program's by a relative error of at most 0.0085.
Values may be sent and summed in bfloat16 or wider, within the bound.
No kernel may reach another device: no remote copies, remote signals or barrier semaphores. Data moves between devices by JAX's collectives and lax.ppermute only.
A program may use at most 256 MiB of HBM per device.

```python
import math
import jax
import jax.numpy as jnp
import numpy as np

D = 6144
FF = 8192
EXPERTS = 4
TOP = 2
TOK_DEV = 16
CAP = 12
TOKENS = 128
N_TOK = 8


def draw_merge_labels(key, part):
    order = jax.random.permutation(key, EXPERTS)
    position = jnp.argsort(order, stable=True)
    return (position // 2).astype(jnp.int32)


def touch_ends(drawn, own_key, low, top_value):
    place = [jax.random.randint(jax.random.fold_in(own_key, axis), (), 0, length) for axis, length in enumerate(drawn.shape)]
    longest = drawn.shape.index(max(drawn.shape))
    next_to = place[:longest] + [(place[longest] + 1) % drawn.shape[longest]] + place[longest + 1:]
    return drawn.at[tuple(place)].set(low).at[tuple(next_to)].set(top_value)


def shard_levels(rng, shape, pieces, smallest, high):
    def one(dim, blocks):
        draws = jax.random.uniform(jax.random.fold_in(jax.random.fold_in(rng, 6), dim), (blocks,), jnp.float32, smallest / len(pieces), high / len(pieces))
        return jnp.repeat(jnp.exp(draws), shape[dim] // blocks).reshape((-1,) + (1,) * (len(shape) - dim - 1))

    gain = one(*pieces[0])
    for cut in pieces[1:]:
        gain = gain * one(*cut)
    return gain


def deal_out(rng, own, number, rows, number_of, top, most, slope):
    sequence = jax.random.permutation(rng, number_of)
    crowded, ordinary = shares(number_of, rows * top, most, slope, True), shares(number_of, rows * top, most, slope, False)
    places = jnp.arange(number_of)

    def named(sizes, offset_by):
        used = int((sizes > 0).sum())
        fixed = max(1, used // 4)
        moved = fixed + (places - fixed + offset_by * (used - fixed)) % max(1, number_of - fixed)
        return jnp.zeros((number_of,), jnp.int32).at[sequence[jnp.where(places < fixed, places, moved)]].set(jnp.asarray(sizes, jnp.int32))

    sizes = jnp.where(number % 4 == 0, named(crowded, number // 4), named(ordinary, number - number // 4 - 1))
    mixed = jax.random.permutation(jax.random.fold_in(own, 3), number_of)
    giver, taker = mixed[0:number_of // 2 * 2:2], mixed[1:number_of // 2 * 2:2]
    margin = jnp.minimum(sizes[giver] - 1, most - sizes[taker]) // 2
    margin = jnp.where((giver == sequence[0]) | (taker == sequence[0]) | (sizes[taker] == 0), 0, jnp.maximum(margin, 0))
    moved = jax.random.randint(jax.random.fold_in(own, 4), (number_of // 2,), 0, 1 << 20) % (margin + 1)
    sizes = sizes.at[giver].add(-moved).at[taker].add(moved)
    items = jnp.searchsorted(jnp.cumsum(sizes), jnp.arange(rows * top), side="right").astype(jnp.int32)
    listing = items.reshape(top, rows).T
    listing = listing[jax.random.permutation(jax.random.fold_in(own, 1), rows)]
    offset_by = jax.random.randint(jax.random.fold_in(own, 2), (rows, 1), 0, top)
    return jnp.take_along_axis(listing, (jnp.arange(top)[None, :] + offset_by) % top, axis=1)


def shares(count, total, limit, skew, full):
    loads = [(1 << 20) // math.isqrt(grade ** skew) + 1 for grade in range(1, count + 1)]
    largest = limit if full else min(limit, max(-(-total // count), total * loads[0] // sum(loads)))
    least = 1 if total - largest >= count - 1 else 0
    counts, spare = [largest] + [least] * (count - 1), total - largest - least * (count - 1)
    while spare > 0:
        movable = [i for i in range(1, count) if counts[i] < largest] or [i for i in range(1, count) if counts[i] < limit]
        pool, budget = sum([loads[i] for i in movable]), spare
        for i in movable:
            addition = min(limit - counts[i], max(1, budget * loads[i] // pool), spare)
            counts[i] = counts[i] + addition
            spare = spare - addition
    return np.array(counts)


def scatter_about(rng, dims, width, bound, cuts=(), held_as=jnp.bfloat16):
    entries = jax.random.normal(rng, dims, jnp.float32) * width
    if len(cuts) > 0:
        entries = shard_levels(rng, dims, cuts, -0.22, 0.18) * entries
    return jnp.clip(entries, min=-bound, max=bound).astype(held_as)


def setup_inputs(seed: int = 0) -> dict:
    key_list = jax.random.split(jax.random.key(seed), 9)
    tokens = scatter_about(key_list[0], (TOKENS, D), 1.0, 6.0, ((0, 8), (1, 4)))
    route_ids_keys = jax.random.split(jax.random.fold_in(key_list[1], 1), TOKENS // TOK_DEV)
    route_ids_turns = jax.random.permutation(jax.random.fold_in(key_list[1], 3), TOKENS // TOK_DEV)
    route_ids = jax.vmap(lambda own, number: deal_out(jax.random.fold_in(key_list[1], 2), own, number, TOK_DEV, EXPERTS, TOP, CAP, 2))(route_ids_keys, route_ids_turns).reshape((TOKENS, TOP))
    gate_codes = touch_ends(jax.random.randint(key_list[2], (TOKENS, TOP), 1, 256), jax.random.fold_in(key_list[2], 1), 1, 255).astype(jnp.int32)
    merge_labels = draw_merge_labels(jax.random.fold_in(key_list[8], 71), 0)
    freq_counts = touch_ends(jax.random.randint(key_list[4], (EXPERTS,), 1024, 4097), jax.random.fold_in(key_list[4], 1), 1024, 4096).astype(jnp.int32)
    w_gate = scatter_about(key_list[5], (EXPERTS * FF, D), D ** -0.5, 0.078125, ((0, 32),))
    w_up = scatter_about(key_list[6], (EXPERTS * FF, D), D ** -0.5, 0.078125, ((0, 32),))
    w_down = scatter_about(key_list[7], (EXPERTS * FF, D), FF ** -0.5, 0.0625, ((0, 8), (1, 4)))
    return {"tokens": tokens, "route_ids": route_ids, "gate_codes": gate_codes, "merge_labels": merge_labels, "freq_counts": freq_counts, "w_gate": w_gate, "w_up": w_up, "w_down": w_down}


def slots_of(route_ids):
    flat = route_ids.reshape(N_TOK, TOK_DEV * TOP)
    picked = (flat[..., None] == jnp.arange(EXPERTS, dtype=jnp.int32)).astype(jnp.int32)
    before = jnp.cumsum(picked, axis=1) - picked
    return jnp.sum(before * picked, axis=2).reshape(N_TOK * TOK_DEV, TOP).astype(jnp.int32)


def swiglu(rows, gate_w, up_w, down_w):
    gate = jnp.dot(rows, gate_w.T, preferred_element_type=jnp.float32)
    upper = jnp.dot(rows, up_w.T, preferred_element_type=jnp.float32)
    hidden = (jax.nn.silu(gate) * upper).astype(jnp.bfloat16)
    return jnp.dot(hidden, down_w, preferred_element_type=jnp.float32)


def reference(tokens, route_ids, gate_codes, merge_labels, freq_counts, w_gate, w_up, w_down):
    slot = slots_of(route_ids)
    shard = (jnp.arange(N_TOK * TOK_DEV, dtype=jnp.int32) // TOK_DEV)[:, None]
    position = (shard * CAP + slot).astype(jnp.int32)
    scale = gate_codes.astype(jnp.float32) / 256.0
    freq = freq_counts.astype(jnp.float32)
    total_rows = N_TOK * CAP
    orig_acc = jnp.zeros((N_TOK * TOK_DEV, D), jnp.float32)
    merged_acc = jnp.zeros((N_TOK * TOK_DEV, D), jnp.float32)
    for expert in range(EXPERTS):
        chosen = route_ids == expert
        target = jnp.where(chosen, position, total_rows).astype(jnp.int32)
        rows = jnp.zeros((total_rows + 1, D), jnp.bfloat16)
        rows = rows.at[target.reshape(-1)].set(jnp.repeat(tokens, TOP, axis=0))[:total_rows]
        member = jnp.where(merge_labels == merge_labels[expert], freq, jnp.float32(0.0))
        coef = member / jnp.sum(member)
        merged = []
        for which in range(3):
            accum = jnp.zeros((FF, D), jnp.float32)
            for other in range(EXPERTS):
                if which == 0:
                    block = w_gate[other * FF:(other + 1) * FF, :]
                elif which == 1:
                    block = w_up[other * FF:(other + 1) * FF, :]
                else:
                    block = w_down[other * FF:(other + 1) * FF, :]
                accum = accum + coef[other] * block.astype(jnp.float32)
            merged.append(accum.astype(jnp.bfloat16))
        y_orig = swiglu(rows, w_gate[expert * FF:(expert + 1) * FF, :], w_up[expert * FF:(expert + 1) * FF, :], w_down[expert * FF:(expert + 1) * FF, :])
        y_merged = swiglu(rows, merged[0], merged[1], merged[2])
        safe = jnp.minimum(target, total_rows - 1)
        weight = jnp.where(chosen, scale, jnp.float32(0.0))[:, :, None]
        orig_acc = orig_acc + jnp.sum(weight * y_orig[safe], axis=1)
        merged_acc = merged_acc + jnp.sum(weight * y_merged[safe], axis=1)
    return orig_acc.astype(jnp.bfloat16), merged_acc.astype(jnp.bfloat16)
```

```python
import functools

import jax
import jax.numpy as jnp
from jax import lax
from jax.experimental import pallas as pl
from jax.experimental.pallas import tpu as pltpu
from jax.sharding import PartitionSpec as P

EXPERTS = 4
TOP = 2
CAP = 12
LANES = 128
UNITS = 256
VMEM_LIMIT = 16 << 20
F32 = jnp.float32
BF16 = jnp.bfloat16
NT = (((1,), (1,)), ((), ()))
IN_VMEM = pl.BlockSpec(memory_space=pltpu.VMEM)
IN_SMEM = pl.BlockSpec(memory_space=pltpu.SMEM)


def swapped(value, axis, by):
    devices = lax.axis_size(axis)
    return lax.ppermute(value, axis, [(i, i ^ by) for i in range(devices)])


def column(table, index):
    lane = lax.broadcasted_iota(jnp.int32, table.shape, 1)
    return jnp.sum(jnp.where(lane == index, table, 0.0), axis=1, keepdims=True)


def silu(v):
    return v / (1.0 + jnp.exp(-v))


def project_kernel(place, x, meta, gate_w, up_w, slots, acts, *, shard, n_exp):
    z, expert = place[0], place[1]
    tokens = x.shape[0]
    depth = x.shape[1] // n_exp
    units = gate_w.shape[0]
    step = min(UNITS, units)
    table = meta[...].astype(F32).T
    line = lax.broadcasted_iota(jnp.int32, table.shape, 0)
    slot = jnp.sum(jnp.where(line == expert, table, 0.0), axis=0, keepdims=True)
    token = lax.broadcasted_iota(jnp.int32, (1, tokens), 1)
    target = jnp.where(slot < 0, -1, (token // shard) * CAP + slot.astype(jnp.int32))
    rows = slots.shape[0]
    pick = (lax.broadcasted_iota(jnp.int32, (rows, tokens), 0) == target).astype(F32).astype(BF16)
    for first in range(0, units, step):
        sums = []
        for weight in (gate_w, up_w):
            total = None
            for k in range(n_exp):
                at = pl.multiple_of((z ^ k) * depth, LANES)
                part = lax.dot_general(
                    weight[first:first + step, pl.ds(at, depth)],
                    x[:, k * depth:(k + 1) * depth],
                    NT,
                    preferred_element_type=F32,
                )
                total = part if total is None else total + part
            sums.append(total)
        gate, upper = sums
        acts[0, first:first + step, :] = gate.astype(BF16)
        acts[1, first:first + step, :] = upper.astype(BF16)
        hidden = (silu(gate) * upper).T.astype(BF16)
        slots[:, first:first + step] = jnp.dot(
            pick, hidden, preferred_element_type=F32
        ).astype(BF16)


def merge_kernel(coefs, own, peer, hidden, *, flip):
    tokens = own.shape[2]
    i = lax.broadcasted_iota(jnp.int32, (tokens, tokens), 0)
    j = lax.broadcasted_iota(jnp.int32, (tokens, tokens), 1)
    order = ((i ^ flip) == j).astype(F32).astype(BF16)
    mixed = []
    for which in range(2):
        theirs = jnp.dot(peer[which], order, preferred_element_type=F32)
        mixed.append(coefs[0] * own[which].astype(F32) + coefs[1] * theirs)
    hidden[...] = (silu(mixed[0]) * mixed[1]).T.astype(BF16)


def down_kernel(place, scale, meta, *refs, shard, packed):
    pieces, weight, out = refs[:-2], refs[-2], refs[-1]
    z, expert, other = place[0], place[1], place[2]
    n_exp = len(pieces)
    depth = weight.shape[0] // n_exp
    table = meta[...].astype(F32)
    tokens = table.shape[0]
    if packed:
        slot = column(table, expert)
        token = lax.broadcasted_iota(jnp.int32, (tokens, 1), 0)
        target = jnp.where(slot < 0, -1, (token // shard) * CAP + slot.astype(jnp.int32))
        rows = pieces[0].shape[0]
        spread = (lax.broadcasted_iota(jnp.int32, (tokens, rows), 1) == target).astype(F32).astype(BF16)
        factor = column(table, EXPERTS + expert)
    else:
        factor = (column(table, EXPERTS + expert) + column(table, EXPERTS + other)) * scale[0]
    total = None
    for k in range(n_exp):
        at = pl.multiple_of((z ^ k) * depth, 16)
        hidden = pieces[k][...]
        if packed:
            hidden = jnp.dot(spread, hidden, preferred_element_type=F32).astype(BF16)
        part = jnp.dot(hidden, weight[pl.ds(at, depth), :], preferred_element_type=F32)
        total = part if total is None else total + part
    out[...] = (total * factor).astype(out.dtype)


def params():
    return pltpu.CompilerParams(vmem_limit_bytes=VMEM_LIMIT)


def spread(value):
    devices = lax.axis_size("exp")
    return (value,) + tuple(swapped(value, "exp", k) for k in range(1, devices))


def exchange(pairing, coefs, slots, acts, *, shard):
    n_tok = lax.axis_size("tok")
    span = n_tok // EXPERTS
    units, all_tokens = acts.shape[1], acts.shape[2]
    with jax.named_scope("peer"):
        peer = swapped(acts, "tok", pairing * span)
    with jax.named_scope("spread_first"):
        first = spread(slots)
    hidden = pl.pallas_call(
        functools.partial(merge_kernel, flip=pairing * span // 2 * shard),
        in_specs=[IN_SMEM, IN_VMEM, IN_VMEM],
        out_specs=IN_VMEM,
        out_shape=jax.ShapeDtypeStruct((all_tokens, units), BF16),
        compiler_params=params(),
        name="merge",
    )(coefs, acts, peer)
    with jax.named_scope("spread_second"):
        second = spread(hidden)
    return first, second


def local(tokens, route_ids, gate_codes, merge_labels, freq_counts, w_gate, w_up, w_down):
    n_tok = lax.axis_size("tok")
    n_exp = lax.axis_size("exp")
    span = n_tok // EXPERTS
    t = lax.axis_index("tok")
    z = lax.axis_index("exp")
    expert = t // span
    shard = tokens.shape[0]
    all_tokens = n_tok * shard
    units = w_gate.shape[0]
    width = w_down.shape[1]
    experts = jnp.arange(EXPERTS, dtype=jnp.int32)
    flat = route_ids.reshape(-1)
    picked = flat[:, None] == experts[None, :]
    earlier = jnp.arange(shard * TOP)[:, None] > jnp.arange(shard * TOP)[None, :]
    before = jnp.sum(
        (earlier[:, :, None] & picked[None, :, :]).astype(F32), axis=1
    )
    slot = jnp.max(jnp.where(picked, before, -1.0).reshape(shard, TOP, EXPERTS), axis=1)
    scale = jnp.sum(
        jnp.where(
            route_ids[:, :, None] == experts[None, None, :],
            gate_codes.astype(F32)[:, :, None] / 256.0,
            0.0,
        ),
        axis=1,
    )
    notes = jnp.concatenate(
        [slot, scale, jnp.zeros((shard, LANES - 2 * EXPERTS), F32)], axis=1
    ).astype(BF16)
    mate = jnp.sum(
        jnp.where((merge_labels == merge_labels[0]) & (experts > 0), experts, 0)
    )
    freq = freq_counts.astype(F32)
    mine = jnp.sum(jnp.where(experts == expert, freq, 0.0))
    theirs = jnp.sum(jnp.where(experts == (expert ^ mate), freq, 0.0))
    coefs = jnp.stack([mine, theirs]) / (mine + theirs)
    place = jnp.stack([z, expert, expert ^ mate]).astype(jnp.int32)

    with jax.named_scope("gather_tokens"):
        row = jnp.concatenate(
            [tokens] + [swapped(tokens, "exp", k) for k in range(1, n_exp)] + [notes], axis=1
        )
        half = jnp.concatenate(
            [row] + [swapped(row, "tok", j) for j in range(2, n_tok, 2)], axis=0
        )
        rows = jnp.concatenate([half, swapped(half, "tok", 1)], axis=0)
        x = rows[:, :-LANES]
        meta = rows[:, -LANES:]

    slots, acts = pl.pallas_call(
        functools.partial(project_kernel, shard=shard, n_exp=n_exp),
        in_specs=[IN_SMEM] + [IN_VMEM] * 4,
        out_specs=[IN_VMEM, IN_VMEM],
        out_shape=[
            jax.ShapeDtypeStruct((n_tok * CAP, units), BF16),
            jax.ShapeDtypeStruct((2, units, all_tokens), BF16),
        ],
        compiler_params=params(),
        name="project",
    )(place, x, meta, w_gate, w_up)
    first, second = lax.switch(
        mate - 1,
        [functools.partial(exchange, pairing, shard=shard) for pairing in range(1, EXPERTS)],
        coefs,
        slots,
        acts,
    )

    def down(pieces, packed):
        return pl.pallas_call(
            functools.partial(down_kernel, shard=shard, packed=packed),
            in_specs=[IN_SMEM, IN_SMEM] + [IN_VMEM] * (len(pieces) + 2),
            out_specs=IN_VMEM,
            out_shape=jax.ShapeDtypeStruct((all_tokens, width), BF16),
            compiler_params=params(),
            name="down",
        )(place, coefs, meta, *pieces, w_down)

    outs = []
    for pieces, packed in ((first, True), (second, False)):
        part = down(pieces, packed)
        middle = all_tokens // 2
        with jax.named_scope("cores"):
            both = part[:middle].astype(F32) + swapped(part[middle:], "tok", 1).astype(F32)
        with jax.named_scope("chips"):
            total = both[:shard]
            sent = both.astype(BF16)
            for i in range(1, n_tok // 2):
                total = total + swapped(sent[i * shard:(i + 1) * shard], "tok", 2 * i).astype(F32)
        outs.append(total.astype(BF16))
    return tuple(outs)


def solution(mesh):
    return jax.shard_map(
        local,
        mesh=mesh,
        in_specs=(
            P("tok", "exp"),
            P("tok", None),
            P("tok", None),
            P(),
            P(),
            P(("tok", "exp"), None),
            P(("tok", "exp"), None),
            P("tok", "exp"),
        ),
        out_specs=(P("tok", "exp"), P("tok", "exp")),
        check_vma=False,
    )
```

```python
import functools

import jax
import jax.numpy as jnp
from jax import lax
from jax.experimental import pallas as pl
from jax.experimental.pallas import tpu as pltpu
from jax.sharding import PartitionSpec as P

EXPERTS = 4
TOP = 2
CAP = 12
LANES = 128
VMEM_LIMIT = 6 << 20
LOADS = 4
F32 = jnp.float32
BF16 = jnp.bfloat16
NT = (((1,), (1,)), ((), ()))
IN_VMEM = pl.BlockSpec(memory_space=pltpu.VMEM)
IN_SMEM = pl.BlockSpec(memory_space=pltpu.SMEM)
IN_HBM = pl.BlockSpec(memory_space=pltpu.HBM)
ANYWHERE = pl.BlockSpec(memory_space=pl.ANY)


def swapped(value, axis, by):
    devices = lax.axis_size(axis)
    return lax.ppermute(value, axis, [(i, i ^ by) for i in range(devices)])


def iota(shape, dim):
    return lax.broadcasted_iota(jnp.int32, shape, dim)


def one_hot(mask):
    return mask.astype(F32).astype(BF16)


def token_flip(tokens, by):
    shape = (tokens, tokens)
    return one_hot((iota(shape, 0) ^ by) == iota(shape, 1))


def silu(v):
    return v / (1.0 + jnp.exp(-v))


def mate_of(labels):
    mate = 0
    for i in range(1, EXPERTS):
        mate = mate + jnp.where(labels[i] == labels[0], i, 0)
    return mate


def notes_kernel(ids, codes, *refs):
    notes = refs[-1]
    shard = ids.shape[1]
    shape = (LANES, shard)
    line = iota(shape, 0)
    picked = jnp.zeros(shape, F32)
    scale = jnp.zeros(shape, F32)
    for k in range(TOP):
        own = ids[k:k + 1, :]
        picked = picked + (own == line).astype(F32)
        weight = codes[k:k + 1, :].astype(F32) / 256.0
        scale = scale + jnp.where(own == line - EXPERTS, weight, 0.0)
    square = (shard, shard)
    earlier = (iota(square, 0) < iota(square, 1)).astype(F32)
    same = (iota(square, 0) == iota(square, 1)).astype(F32)
    slot = jnp.dot(picked, earlier, preferred_element_type=F32)
    slot = jnp.where(picked > 0.0, slot, -1.0)
    table = jnp.where(line < EXPERTS, slot, scale)
    notes[...] = lax.dot_general(same, table, NT, preferred_element_type=F32).astype(BF16)


def load_kernel(place, *refs, ks):
    weights, (blocks, done, sems) = refs[:2], refs[-3:]
    rows = blocks.shape[2] // LOADS
    depth = blocks.shape[3]
    copies = []
    for i, k in enumerate(ks):
        columns = pl.ds(pl.multiple_of((place[0] ^ k) * depth, LANES), depth)
        for w, weight in enumerate(weights):
            for p in range(LOADS):
                part = pl.ds(p * rows, rows)
                copies.append(
                    pltpu.make_async_copy(
                        weight.at[part, columns], blocks.at[w, i, part], sems.at[w, i, p]
                    )
                )
    for copy in copies:
        copy.start()
    for copy in copies:
        copy.wait()
    done[...] = jnp.zeros(done.shape, F32)


def product(place, blocks, x, j, w):
    size = blocks.shape[2] // EXPERTS
    depth = blocks.shape[3]
    rows = pl.ds(pl.multiple_of((place[1] ^ j) * size, 16), size)
    total = None
    for i in range(blocks.shape[1]):
        part = lax.dot_general(
            blocks[w, i, rows], x[:, i * depth:(i + 1) * depth], NT, preferred_element_type=F32
        )
        total = part if total is None else total + part
    return total


def project_first_kernel(place, x, blocks, *refs):
    sums = refs[-1]
    for j in range(EXPERTS):
        for w in range(2):
            sums[j, w] = product(place, blocks, x, j, w)


def picks(notes, expert, rows, shard):
    table = notes[...].astype(F32).T
    slot = jnp.sum(jnp.where(iota(table.shape, 0) == expert, table, 0.0), axis=0, keepdims=True)
    tokens = slot.shape[1]
    first = (iota((1, tokens), 1) // shard) * CAP
    target = jnp.where(slot < 0.0, -1, first + slot.astype(jnp.int32))
    return one_hot(iota((rows, tokens), 0) == target)


def project_sent_kernel(place, x, notes, sums, blocks, slots, *sent, shard):
    size = blocks.shape[2] // EXPERTS
    pick = picks(notes, place[1], slots.shape[0], shard)
    for j in range(1, EXPERTS):
        gate = product(place, blocks, x, j, 0) + sums[j, 0]
        upper = product(place, blocks, x, j, 1) + sums[j, 1]
        sent[j - 1][0] = gate.astype(BF16)
        sent[j - 1][1] = upper.astype(BF16)
        hidden = (silu(gate) * upper).T.astype(BF16)
        slots[:, (j - 1) * size:j * size] = jnp.dot(
            pick, hidden, preferred_element_type=F32
        ).astype(BF16)


def project_own_kernel(place, x, notes, sums, blocks, others, slots, own, *, shard):
    size = blocks.shape[2] // EXPERTS
    pick = picks(notes, place[1], slots.shape[0], shard)
    gate = product(place, blocks, x, 0, 0) + sums[0, 0]
    upper = product(place, blocks, x, 0, 1) + sums[0, 1]
    own[0] = gate
    own[1] = upper
    hidden = (silu(gate) * upper).T.astype(BF16)
    slots[:, :size] = jnp.dot(pick, hidden, preferred_element_type=F32).astype(BF16)
    slots[:, size:] = others[...]


def merge_kernel(place, labels, freq, own, *refs, flips):
    peers, hidden = refs[:EXPERTS - 1], refs[-1]
    expert = place[1]
    mate = mate_of(labels)
    tokens = own.shape[2]
    parts = [own]
    counts = [jnp.full((1, 1), freq[expert], jnp.int32).astype(F32)]
    for j, peer in enumerate(peers, 1):
        order = token_flip(tokens, flips[j - 1])
        parts.append([jnp.dot(peer[i], order, preferred_element_type=F32) for i in range(2)])
        counts.append(jnp.full((1, 1), freq[expert ^ j], jnp.int32).astype(F32))
    for group in range(2):
        member = []
        for j in range(EXPERTS):
            same = jnp.logical_or(j == 0, mate == j)
            member.append(jnp.where(same if group == 0 else jnp.logical_not(same), counts[j], 0.0))
        whole = member[0] + member[1] + member[2] + member[3]
        gate, upper = [
            sum((member[j] / whole) * parts[j][i] for j in range(EXPERTS)) for i in range(2)
        ]
        hidden[group] = (silu(gate) * upper).T.astype(BF16)


def route_kernel(labels, *refs, count):
    pieces, sent = refs[:count], refs[1 - EXPERTS:]
    mate = mate_of(labels)
    for j, to in enumerate(sent, 1):
        group = jnp.where(mate == j, 0, 1)
        for i in range(count):
            to[i] = pieces[i][group]


def times_weight(place, weight, hidden, ks, n_exp, factor, store):
    z, expert = place[0], place[1]
    depth = weight.shape[0] // n_exp
    size = depth // EXPERTS
    width = weight.shape[1]
    step = min(256, width)
    for n in range(0, width, step):
        total = None
        for i, k in enumerate(ks):
            for j in range(EXPERTS):
                at = pl.multiple_of((z ^ k) * depth + (expert ^ j) * size, 16)
                part = jnp.dot(
                    hidden[:, (i * EXPERTS + j) * size:(i * EXPERTS + j + 1) * size],
                    weight[pl.ds(at, size), n:n + step],
                    preferred_element_type=F32,
                )
                total = part if total is None else total + part
        store(n, step, total * factor)


def first_down_kernel(place, notes, *refs, shard, n_exp, line):
    weight, *pieces = refs[:-2]
    out, hidden = refs[-2:]
    z, expert = place[0], place[1]
    depth = weight.shape[0] // n_exp
    ks = list(range(n_exp))
    inner = None
    if line:
        inner = jnp.logical_or(z == 1, z == 2)
        ks = [0, 1, jnp.where(inner, 3, 2), jnp.where(inner, 2, 3)]
        pieces = [[pieces[0]], [pieces[1]], [pieces[2], pieces[4]], [pieces[3], pieces[5]]]
    else:
        pieces = [[piece] for piece in pieces[:n_exp]]
    table = notes[...].astype(F32)
    tokens = table.shape[0]
    lane = iota(table.shape, 1)
    slot = jnp.sum(jnp.where(lane == expert, table, 0.0), axis=1, keepdims=True)
    factor = jnp.sum(jnp.where(lane == EXPERTS + expert, table, 0.0), axis=1, keepdims=True)
    first = (iota((tokens, 1), 0) // shard) * CAP
    target = jnp.where(slot < 0.0, -1, first + slot.astype(jnp.int32))
    spread = one_hot(iota((tokens, pieces[0][0].shape[0]), 1) == target)
    for i, found in enumerate(pieces):
        piece = found[0][...]
        if len(found) > 1:
            piece = jnp.where(inner, piece, found[1][...])
        hidden[:, i * depth:(i + 1) * depth] = jnp.dot(
            spread, piece, preferred_element_type=F32
        ).astype(BF16)

    def store(n, step, total):
        out[:, n:n + step] = total

    times_weight(place, weight, hidden, ks, n_exp, factor, store)


def second_down_kernel(place, labels, freq, notes, weight, initial, *refs, flips, n_exp, shard):
    own, refs = refs[:n_exp], refs[n_exp:]
    peers, (keep, sent, hidden) = refs[:-3], refs[-3:]
    expert = place[1]
    size = weight.shape[0] // n_exp // EXPERTS
    table = notes[...].astype(F32)
    tokens = table.shape[0]
    mate = mate_of(labels)
    lane = iota(table.shape, 1)
    mine = jnp.logical_or(lane == EXPERTS + expert, lane == EXPERTS + (expert ^ mate))
    factor = jnp.sum(jnp.where(mine, table, 0.0), axis=1, keepdims=True)
    chosen = jnp.full((1, 1), freq[expert], jnp.int32).astype(F32)
    other = jnp.full((1, 1), freq[expert ^ mate], jnp.int32).astype(F32)
    factor = factor * (chosen / (chosen + other))
    for j in range(1, EXPERTS):
        order = token_flip(tokens, flips[j - 1])
        found = []
        for part in peers[j - 1::EXPERTS - 1]:
            found += [part[i] for i in range(part.shape[0])]
        for k in range(n_exp):
            at = (k * EXPERTS + j) * size
            hidden[:, at:at + size] = jnp.dot(
                order, found[k], preferred_element_type=F32
            ).astype(BF16)
    for k in range(n_exp):
        hidden[:, k * EXPERTS * size:(k * EXPERTS + 1) * size] = own[k][0]
    middle = tokens // 2

    def put(index, n, step, total):
        for c in range(middle // shard):
            rows = slice(c * shard, (c + 1) * shard)
            keep[c, index, :, n:n + step] = total[rows]
            rows = slice(middle + c * shard, middle + (c + 1) * shard)
            sent[c, index, :, n:n + step] = total[rows].astype(BF16)

    def store(n, step, total):
        put(0, n, step, initial[:, n:n + step])
        put(1, n, step, total)

    times_weight(place, weight, hidden, range(n_exp), n_exp, factor, store)


def cores_kernel(keep, theirs, own, *sent):
    own[...] = keep[0] + theirs[0].astype(F32)
    for c, to in enumerate(sent, 1):
        to[...] = (keep[c] + theirs[c].astype(F32)).astype(BF16)


def finish_kernel(own, *refs):
    parts, outs = refs[:-2], refs[-2:]
    for i, out in enumerate(outs):
        total = own[i]
        for part in parts:
            total = total + part[i].astype(F32)
        out[...] = total.astype(BF16)


def local(tokens, route_ids, gate_codes, merge_labels, freq_counts, w_gate, w_up, w_down):
    n_tok = lax.axis_size("tok")
    n_exp = lax.axis_size("exp")
    span = n_tok // EXPERTS
    z = lax.axis_index("exp")
    expert = lax.axis_index("tok") // span
    shard, depth = tokens.shape
    all_tokens = n_tok * shard
    units = w_gate.shape[0]
    size = units // EXPERTS
    width = w_down.shape[1]
    half = n_exp // 2
    flips = tuple(j * span // 2 * shard for j in range(1, EXPERTS))
    others = range(1, EXPERTS)
    gate_w = pltpu.with_memory_space_constraint(w_gate, pltpu.HBM)
    up_w = pltpu.with_memory_space_constraint(w_up, pltpu.HBM)
    place = jnp.stack([z, expert]).astype(jnp.int32)
    shape = jax.ShapeDtypeStruct

    small = pl.CostEstimate(flops=1, bytes_accessed=1, transcendentals=0)
    limit = VMEM_LIMIT if all_tokens <= LANES else 2 * VMEM_LIMIT

    def call(kernel, name, out_shape, *args, scratch=(), smem=0, unused=0, hbm=0, cost=True):
        specs = [IN_SMEM] * smem + [IN_HBM] * hbm
        specs += [IN_VMEM] * (len(args) - len(specs) - unused) + [ANYWHERE] * unused
        return pl.pallas_call(
            kernel,
            in_specs=specs,
            out_specs=[IN_VMEM] * len(out_shape) if isinstance(out_shape, list) else IN_VMEM,
            out_shape=out_shape,
            scratch_shapes=scratch,
            compiler_params=pltpu.CompilerParams(vmem_limit_bytes=limit),
            cost_estimate=small if cost else None,
            name=name,
        )(*args)

    def load(ks, *after):
        return call(
            functools.partial(load_kernel, ks=ks),
            "load",
            [pltpu.VMEM((2, len(ks), units, depth), BF16), shape((8, LANES), F32)],
            place,
            gate_w,
            up_w,
            *after,
            scratch=[pltpu.SemaphoreType.DMA((2, len(ks), LOADS))],
            smem=1,
            hbm=2,
            unused=len(after),
            cost=False,
        )

    near_w, near_done = load(range(half))
    notes = call(
        notes_kernel, "notes", shape((shard, LANES), BF16), route_ids.T, gate_codes.T, near_done, unused=1
    )

    with jax.named_scope("gather_tokens"):
        rows = [tokens] + [swapped(tokens, "exp", k) for k in range(1, n_exp)]
        near = jnp.concatenate([notes] + rows[:half], axis=1)
        far = jnp.concatenate(rows[half:], axis=1)

        def chips(row):
            return [row] + [swapped(row, "tok", j) for j in range(2, n_tok, 2)]

        def cores(parts):
            rows = jnp.concatenate(parts, axis=0)
            return jnp.concatenate([rows, swapped(rows, "tok", 1)], axis=0), rows

        near = chips(near)
        near[1], far = lax.optimization_barrier((near[1], far))
        far = chips(far)
        near, near_rows = cores(near)
        far_w, far_done = load(range(half, n_exp), near_rows)
        far, _ = cores(far)
        table = near[:, :LANES]
        near = near[:, LANES:]

    sums = call(
        project_first_kernel,
        "project_first",
        shape((EXPERTS, 2, size, all_tokens), F32),
        place,
        near,
        near_w,
        far_done,
        smem=1,
        unused=1,
        cost=False,
    )
    others_slots, *sent = call(
        functools.partial(project_sent_kernel, shard=shard),
        "project_sent",
        [shape((n_tok * CAP, units - size), BF16)]
        + [shape((2, size, all_tokens), BF16) for _ in others],
        place,
        far,
        table,
        sums,
        far_w,
        smem=1,
        cost=False,
    )
    with jax.named_scope("peers"):
        peers = [swapped(sent[j - 1], "tok", j * span) for j in others]
    slots, own = call(
        functools.partial(project_own_kernel, shard=shard),
        "project_own",
        [shape((n_tok * CAP, units), BF16), shape((2, size, all_tokens), F32)],
        place,
        far,
        table,
        sums,
        far_w,
        others_slots,
        smem=1,
        cost=False,
    )
    line = n_exp == 4
    middle = ((1, 2), (2, 1))
    ends = ((1, 0), (2, 3))
    with jax.named_scope("spread_first"):
        if line:
            early = [swapped(slots, "exp", 1), lax.ppermute(slots, "exp", middle)]
        else:
            early = [swapped(slots, "exp", k) for k in range(1, n_exp)]
    merged = call(
        functools.partial(merge_kernel, flips=flips),
        "merge",
        shape((2, all_tokens, size), BF16),
        place,
        merge_labels,
        freq_counts,
        own,
        *peers,
        smem=3,
    )
    with jax.named_scope("spread_second"):
        second = [merged] + [swapped(merged, "exp", k) for k in range(1, n_exp)]
    with jax.named_scope("spread_first"):
        first = [slots] + early
        later = []
        if line:
            later = [lax.ppermute(early[0], "exp", middle), lax.ppermute(early[1], "exp", ends)]
            later[0], second[1] = lax.optimization_barrier((later[0], second[1]))
            first += later + [lax.ppermute(later[0], "exp", ends)]

    def grouped(pieces, *after):
        out = call(
            functools.partial(route_kernel, count=len(pieces)),
            "route",
            [shape((len(pieces), all_tokens, size), BF16) for _ in others],
            merge_labels,
            *pieces,
            *after,
            smem=1,
            unused=len(after),
        )
        with jax.named_scope("groups"):
            return out, [swapped(out[j - 1], "tok", j * span) for j in others]

    own_out, groups = grouped(second[:1], second[1])
    far_out, more = grouped(second[1:], *groups)
    initial = call(
        functools.partial(first_down_kernel, shard=shard, n_exp=n_exp, line=line),
        "first_down",
        shape((all_tokens, width), F32),
        place,
        table,
        w_down,
        *first,
        far_out[0],
        scratch=[pltpu.VMEM((all_tokens, n_exp * units), BF16)],
        smem=1,
        unused=1,
        cost=False,
    )
    ends = (n_tok // 2, 2, shard, width)
    keep, sent = call(
        functools.partial(second_down_kernel, flips=flips, n_exp=n_exp, shard=shard),
        "second_down",
        [shape(ends, F32), shape(ends, BF16)],
        place,
        merge_labels,
        freq_counts,
        table,
        w_down,
        initial,
        *second,
        *groups,
        *more,
        scratch=[pltpu.VMEM((all_tokens, n_exp * units), BF16)],
        smem=3,
        cost=False,
    )
    with jax.named_scope("cores"):
        theirs = swapped(sent, "tok", 1)
    piece = (2, shard, width)
    own, *sent = call(
        cores_kernel,
        "cores",
        [shape(piece, F32)] + [shape(piece, BF16) for _ in range(1, n_tok // 2)],
        keep,
        theirs,
    )
    with jax.named_scope("chips"):
        parts = [swapped(value, "tok", 2 * c) for c, value in enumerate(sent, 1)]
    return tuple(
        call(finish_kernel, "finish", [shape((shard, width), BF16)] * 2, own, *parts)
    )


def solution(mesh):
    return jax.shard_map(
        local,
        mesh=mesh,
        in_specs=(
            P("tok", "exp"),
            P("tok", None),
            P("tok", None),
            P(),
            P(),
            P(("tok", "exp"), None),
            P(("tok", "exp"), None),
            P("tok", "exp"),
        ),
        out_specs=(P("tok", "exp"), P("tok", "exp")),
        check_vma=False,
    )
```

```python
import functools

import jax
import jax.numpy as jnp
from jax import lax
from jax.experimental import pallas as pl
from jax.experimental.pallas import tpu as pltpu
from jax.sharding import PartitionSpec as P

EXPERTS = 4
TOP = 2
CAP = 12
LANES = 128
VMEM_LIMIT = 6 << 20
LOADS = 4
F32 = jnp.float32
BF16 = jnp.bfloat16
NT = (((1,), (1,)), ((), ()))
IN_VMEM = pl.BlockSpec(memory_space=pltpu.VMEM)
IN_SMEM = pl.BlockSpec(memory_space=pltpu.SMEM)
IN_HBM = pl.BlockSpec(memory_space=pltpu.HBM)
ANYWHERE = pl.BlockSpec(memory_space=pl.ANY)


def swapped(value, axis, by):
    devices = lax.axis_size(axis)
    return lax.ppermute(value, axis, [(i, i ^ by) for i in range(devices)])


def iota(shape, dim):
    return lax.broadcasted_iota(jnp.int32, shape, dim)


def one_hot(mask):
    return mask.astype(F32).astype(BF16)


def token_flip(tokens, by):
    shape = (tokens, tokens)
    return one_hot((iota(shape, 0) ^ by) == iota(shape, 1))


def silu(v):
    return v / (1.0 + jnp.exp(-v))


def mate_of(labels):
    mate = 0
    for i in range(1, EXPERTS):
        mate = mate + jnp.where(labels[i] == labels[0], i, 0)
    return mate


def notes_kernel(ids, codes, *refs):
    notes = refs[-1]
    shard = ids.shape[1]
    shape = (LANES, shard)
    line = iota(shape, 0)
    picked = jnp.zeros(shape, F32)
    scale = jnp.zeros(shape, F32)
    for k in range(TOP):
        own = ids[k:k + 1, :]
        picked = picked + (own == line).astype(F32)
        weight = codes[k:k + 1, :].astype(F32) / 256.0
        scale = scale + jnp.where(own == line - EXPERTS, weight, 0.0)
    square = (shard, shard)
    earlier = (iota(square, 0) < iota(square, 1)).astype(F32)
    same = (iota(square, 0) == iota(square, 1)).astype(F32)
    slot = jnp.dot(picked, earlier, preferred_element_type=F32)
    slot = jnp.where(picked > 0.0, slot, -1.0)
    table = jnp.where(line < EXPERTS, slot, scale)
    notes[...] = lax.dot_general(same, table, NT, preferred_element_type=F32).astype(BF16)


def load_kernel(place, gate_w, up_w, *refs, ks):
    blocks, done, sems = refs[-3:]
    rows = blocks.shape[2] // LOADS
    depth = blocks.shape[3]
    copies = []
    for i, k in enumerate(ks):
        columns = pl.ds(pl.multiple_of((place[0] ^ k) * depth, LANES), depth)
        for w, weight in enumerate((gate_w, up_w)):
            for p in range(LOADS):
                part = pl.ds(p * rows, rows)
                copies.append(
                    pltpu.make_async_copy(
                        weight.at[part, columns], blocks.at[w, k, part], sems.at[w, i, p]
                    )
                )
    for copy in copies:
        copy.start()
    for copy in copies:
        copy.wait()
    done[...] = jnp.zeros(done.shape, F32)


def load_down_kernel(weight, *refs):
    held, done, sems = refs[-3:]
    rows = weight.shape[0] // (4 * LOADS)
    copies = []
    for p in range(4 * LOADS):
        part = pl.ds(p * rows, rows)
        copies.append(pltpu.make_async_copy(weight.at[part], held.at[part], sems.at[p]))
    for copy in copies:
        copy.start()
    for copy in copies:
        copy.wait()
    done[...] = jnp.zeros(done.shape, F32)


def product(place, blocks, x, j, w):
    size = blocks.shape[2] // EXPERTS
    depth = blocks.shape[3]
    rows = pl.ds(pl.multiple_of((place[1] ^ j) * size, 16), size)
    total = None
    for i in range(blocks.shape[1]):
        part = lax.dot_general(
            blocks[w, i, rows], x[:, LANES + i * depth:LANES + (i + 1) * depth], NT, preferred_element_type=F32
        )
        total = part if total is None else total + part
    return total


def picks(notes, expert, rows, shard):
    table = notes.astype(F32).T
    slot = jnp.sum(jnp.where(iota(table.shape, 0) == expert, table, 0.0), axis=0, keepdims=True)
    tokens = slot.shape[1]
    first = (iota((1, tokens), 1) // shard) * CAP
    target = jnp.where(slot < 0.0, -1, first + slot.astype(jnp.int32))
    return one_hot(iota((rows, tokens), 0) == target)


def project_sent_kernel(place, x, blocks, slots, *sent, shard):
    size = blocks.shape[2] // EXPERTS
    pick = picks(x[:, :LANES], place[1], slots.shape[0], shard)
    for j in range(1, EXPERTS):
        gate = product(place, blocks, x, j, 0)
        upper = product(place, blocks, x, j, 1)
        sent[j - 1][0] = gate.astype(BF16)
        sent[j - 1][1] = upper.astype(BF16)
        hidden = (silu(gate) * upper).T.astype(BF16)
        slots[:, (j - 1) * size:j * size] = jnp.dot(
            pick, hidden, preferred_element_type=F32
        ).astype(BF16)


def project_own_kernel(place, x, blocks, others, slots, own, *, shard):
    size = blocks.shape[2] // EXPERTS
    pick = picks(x[:, :LANES], place[1], slots.shape[0], shard)
    gate = product(place, blocks, x, 0, 0)
    upper = product(place, blocks, x, 0, 1)
    own[0] = gate
    own[1] = upper
    hidden = (silu(gate) * upper).T.astype(BF16)
    slots[:, :size] = jnp.dot(pick, hidden, preferred_element_type=F32).astype(BF16)
    slots[:, size:] = others[...]


def merge_kernel(place, labels, freq, own, *refs, flips):
    peers, hidden = refs[:EXPERTS - 1], refs[-1]
    expert = place[1]
    mate = mate_of(labels)
    tokens = own.shape[2]
    parts = [own]
    counts = [jnp.full((1, 1), freq[expert], jnp.int32).astype(F32)]
    for j, peer in enumerate(peers, 1):
        order = token_flip(tokens, flips[j - 1])
        parts.append([jnp.dot(peer[i], order, preferred_element_type=F32) for i in range(2)])
        counts.append(jnp.full((1, 1), freq[expert ^ j], jnp.int32).astype(F32))
    for group in range(2):
        member = []
        for j in range(EXPERTS):
            same = jnp.logical_or(j == 0, mate == j)
            member.append(jnp.where(same if group == 0 else jnp.logical_not(same), counts[j], 0.0))
        whole = member[0] + member[1] + member[2] + member[3]
        gate, upper = [
            sum((member[j] / whole) * parts[j][i] for j in range(EXPERTS)) for i in range(2)
        ]
        hidden[group] = (silu(gate) * upper).T.astype(BF16)


def route_kernel(labels, *refs, count):
    pieces, sent = refs[:count], refs[1 - EXPERTS:]
    mate = mate_of(labels)
    for j, to in enumerate(sent, 1):
        group = jnp.where(mate == j, 0, 1)
        for i in range(count):
            to[i] = pieces[i][group]


def times_weight(place, weight, hidden, ks, n_exp, factor, store):
    z, expert = place[0], place[1]
    depth = weight.shape[0] // n_exp
    size = depth // EXPERTS
    width = weight.shape[1]
    step = min(256, width)
    for n in range(0, width, step):
        total = None
        for i, k in enumerate(ks):
            for j in range(EXPERTS):
                at = pl.multiple_of((z ^ k) * depth + (expert ^ j) * size, 16)
                part = jnp.dot(
                    hidden[:, (i * EXPERTS + j) * size:(i * EXPERTS + j + 1) * size],
                    weight[pl.ds(at, size), n:n + step],
                    preferred_element_type=F32,
                )
                total = part if total is None else total + part
        store(n, step, total * factor)


def first_down_kernel(place, notes, weight, *refs, shard, n_exp):
    pieces, (out, hidden) = refs[:n_exp], refs[-2:]
    expert = place[1]
    depth = weight.shape[0] // n_exp
    table = notes[...].astype(F32)
    tokens = table.shape[0]
    lane = iota(table.shape, 1)
    slot = jnp.sum(jnp.where(lane == expert, table, 0.0), axis=1, keepdims=True)
    factor = jnp.sum(jnp.where(lane == EXPERTS + expert, table, 0.0), axis=1, keepdims=True)
    first = (iota((tokens, 1), 0) // shard) * CAP
    target = jnp.where(slot < 0.0, -1, first + slot.astype(jnp.int32))
    spread = one_hot(iota((tokens, pieces[0].shape[0]), 1) == target)
    for k, piece in enumerate(pieces):
        hidden[:, k * depth:(k + 1) * depth] = jnp.dot(
            spread, piece[...], preferred_element_type=F32
        ).astype(BF16)

    def store(n, step, total):
        out[:, n:n + step] = total

    times_weight(place, weight, hidden, range(n_exp), n_exp, factor, store)


def second_down_kernel(place, labels, freq, notes, weight, initial, *refs, flips, n_exp, shard):
    own, refs = refs[:n_exp], refs[n_exp:]
    peers, (keep, sent, hidden) = refs[:-3], refs[-3:]
    expert = place[1]
    size = weight.shape[0] // n_exp // EXPERTS
    table = notes[...].astype(F32)
    tokens = table.shape[0]
    mate = mate_of(labels)
    lane = iota(table.shape, 1)
    mine = jnp.logical_or(lane == EXPERTS + expert, lane == EXPERTS + (expert ^ mate))
    factor = jnp.sum(jnp.where(mine, table, 0.0), axis=1, keepdims=True)
    chosen = jnp.full((1, 1), freq[expert], jnp.int32).astype(F32)
    other = jnp.full((1, 1), freq[expert ^ mate], jnp.int32).astype(F32)
    factor = factor * (chosen / (chosen + other))
    for j in range(1, EXPERTS):
        order = token_flip(tokens, flips[j - 1])
        found = []
        for part in peers[j - 1::EXPERTS - 1]:
            found += [part[i] for i in range(part.shape[0])]
        for k in range(n_exp):
            at = (k * EXPERTS + j) * size
            hidden[:, at:at + size] = jnp.dot(
                order, found[k], preferred_element_type=F32
            ).astype(BF16)
    for k in range(n_exp):
        hidden[:, k * EXPERTS * size:(k * EXPERTS + 1) * size] = own[k][0]
    middle = tokens // 2

    def put(index, n, step, total):
        for c in range(middle // shard):
            rows = slice(c * shard, (c + 1) * shard)
            keep[c, index, :, n:n + step] = total[rows]
            rows = slice(middle + c * shard, middle + (c + 1) * shard)
            sent[c, index, :, n:n + step] = total[rows].astype(BF16)

    def store(n, step, total):
        put(0, n, step, initial[:, n:n + step])
        put(1, n, step, total)

    times_weight(place, weight, hidden, range(n_exp), n_exp, factor, store)


def cores_kernel(keep, theirs, own, *sent):
    own[...] = keep[0] + theirs[0].astype(F32)
    for c, to in enumerate(sent, 1):
        to[...] = (keep[c] + theirs[c].astype(F32)).astype(BF16)


def finish_kernel(own, *refs):
    parts, outs = refs[:-2], refs[-2:]
    for i, out in enumerate(outs):
        total = own[i]
        for part in parts:
            total = total + part[i].astype(F32)
        out[...] = total.astype(BF16)


def local(tokens, route_ids, gate_codes, merge_labels, freq_counts, w_gate, w_up, w_down):
    n_tok = lax.axis_size("tok")
    n_exp = lax.axis_size("exp")
    span = n_tok // EXPERTS
    z = lax.axis_index("exp")
    expert = lax.axis_index("tok") // span
    shard, depth = tokens.shape
    all_tokens = n_tok * shard
    units = w_gate.shape[0]
    size = units // EXPERTS
    width = w_down.shape[1]
    half = n_exp // 2
    flips = tuple(j * span // 2 * shard for j in range(1, EXPERTS))
    others = range(1, EXPERTS)
    gate_w = pltpu.with_memory_space_constraint(w_gate, pltpu.HBM)
    up_w = pltpu.with_memory_space_constraint(w_up, pltpu.HBM)
    down_w = pltpu.with_memory_space_constraint(w_down, pltpu.HBM)
    place = jnp.stack([z, expert]).astype(jnp.int32)
    shape = jax.ShapeDtypeStruct

    small = pl.CostEstimate(flops=1, bytes_accessed=1, transcendentals=0)
    limit = VMEM_LIMIT if all_tokens <= LANES else 2 * VMEM_LIMIT

    def call(kernel, name, out_shape, *args, scratch=(), smem=0, unused=0, hbm=0, cost=True):
        specs = [IN_SMEM] * smem + [IN_HBM] * hbm
        specs += [IN_VMEM] * (len(args) - len(specs) - unused) + [ANYWHERE] * unused
        return pl.pallas_call(
            kernel,
            in_specs=specs,
            out_specs=[IN_VMEM] * len(out_shape) if isinstance(out_shape, list) else IN_VMEM,
            out_shape=out_shape,
            scratch_shapes=scratch,
            compiler_params=pltpu.CompilerParams(vmem_limit_bytes=limit),
            cost_estimate=small if cost else None,
            name=name,
        )(*args)

    def load(ks, before=None, *after):
        aliased = [] if before is None else [before]
        blocks = (2, n_exp, units, depth)
        return pl.pallas_call(
            functools.partial(load_kernel, ks=ks),
            in_specs=[IN_SMEM, IN_HBM, IN_HBM]
            + [IN_VMEM] * len(aliased)
            + [ANYWHERE] * len(after),
            out_specs=[IN_VMEM] * 2,
            out_shape=[pltpu.VMEM(blocks, BF16), shape((8, LANES), F32)],
            scratch_shapes=[pltpu.SemaphoreType.DMA((2, len(ks), LOADS))],
            input_output_aliases={3: 0} if aliased else {},
            compiler_params=pltpu.CompilerParams(vmem_limit_bytes=limit),
            name="load",
        )(place, gate_w, up_w, *aliased, *after)

    weights, done = load(range(half))
    notes = call(
        notes_kernel,
        "notes",
        shape((shard, LANES), BF16),
        route_ids.T,
        gate_codes.T,
        done,
        unused=1,
    )
    with jax.named_scope("gather_tokens"):
        row = jnp.concatenate(
            [notes, tokens] + [swapped(tokens, "exp", k) for k in range(1, n_exp)], axis=1
        )
        weights, _ = load(range(half, n_exp), weights, row)
        chips = jnp.concatenate(
            [row] + [swapped(row, "tok", j) for j in range(2, n_tok, 2)], axis=0
        )
        x = jnp.concatenate([chips, swapped(chips, "tok", 1)], axis=0)
        table = x[:, :LANES]

    others_slots, *sent = call(
        functools.partial(project_sent_kernel, shard=shard),
        "project_sent",
        [shape((n_tok * CAP, units - size), BF16)]
        + [shape((2, size, all_tokens), BF16) for _ in others],
        place,
        x,
        weights,
        smem=1,
        cost=False,
    )
    with jax.named_scope("peers"):
        peers = [swapped(sent[j - 1], "tok", j * span) for j in others]
    slots, own = call(
        functools.partial(project_own_kernel, shard=shard),
        "project_own",
        [shape((n_tok * CAP, units), BF16), shape((2, size, all_tokens), F32)],
        place,
        x,
        weights,
        others_slots,
        smem=1,
        cost=False,
    )
    early = n_exp // 2
    with jax.named_scope("spread_first"):
        sooner = swapped(slots, "exp", early)
    merged = call(
        functools.partial(merge_kernel, flips=flips),
        "merge",
        shape((2, all_tokens, size), BF16),
        place,
        merge_labels,
        freq_counts,
        own,
        *peers,
        sooner,
        smem=3,
        unused=1,
    )
    with jax.named_scope("spread_second"):
        second = [merged] + [swapped(merged, "exp", k) for k in range(1, n_exp)]
    def grouped(pieces, *after):
        out = call(
            functools.partial(route_kernel, count=len(pieces)),
            "route",
            [shape((len(pieces), all_tokens, size), BF16) for _ in others],
            merge_labels,
            *pieces,
            *after,
            smem=1,
            unused=len(after),
        )
        with jax.named_scope("groups"):
            return out, [swapped(out[j - 1], "tok", j * span) for j in others]

    down_v, down_done = call(
        load_down_kernel,
        "load_down",
        [pltpu.VMEM(w_down.shape, BF16), shape((8, LANES), F32)],
        down_w,
        second[1],
        scratch=[pltpu.SemaphoreType.DMA((4 * LOADS,))],
        hbm=1,
        unused=1,
        cost=False,
    )
    own_out, groups = grouped(second[:1], down_done)
    waiting, _ = lax.optimization_barrier((slots, down_done))
    with jax.named_scope("spread_first"):
        first = [slots] + [
            sooner if k == early else swapped(waiting, "exp", k) for k in range(1, n_exp)
        ]
    far_out, more = grouped(second[1:], *groups)
    initial = call(
        functools.partial(first_down_kernel, shard=shard, n_exp=n_exp),
        "first_down",
        shape((all_tokens, width), F32),
        place,
        table,
        down_v,
        *first,
        far_out[0],
        scratch=[pltpu.VMEM((all_tokens, n_exp * units), BF16)],
        smem=1,
        unused=1,
        cost=False,
    )
    ends = (n_tok // 2, 2, shard, width)
    keep, sent = call(
        functools.partial(second_down_kernel, flips=flips, n_exp=n_exp, shard=shard),
        "second_down",
        [shape(ends, F32), shape(ends, BF16)],
        place,
        merge_labels,
        freq_counts,
        table,
        down_v,
        initial,
        *second,
        *groups,
        *more,
        scratch=[pltpu.VMEM((all_tokens, n_exp * units), BF16)],
        smem=3,
        cost=False,
    )
    with jax.named_scope("cores"):
        theirs = swapped(sent, "tok", 1)
    piece = (2, shard, width)
    own, *sent = call(
        cores_kernel,
        "cores",
        [shape(piece, F32)] + [shape(piece, BF16) for _ in range(1, n_tok // 2)],
        keep,
        theirs,
    )
    with jax.named_scope("chips"):
        parts = [swapped(value, "tok", 2 * c) for c, value in enumerate(sent, 1)]
    return tuple(
        call(finish_kernel, "finish", [shape((shard, width), BF16)] * 2, own, *parts)
    )


def solution(mesh):
    return jax.shard_map(
        local,
        mesh=mesh,
        in_specs=(
            P("tok", "exp"),
            P("tok", None),
            P("tok", None),
            P(),
            P(),
            P(("tok", "exp"), None),
            P(("tok", "exp"), None),
            P("tok", "exp"),
        ),
        out_specs=(P("tok", "exp"), P("tok", "exp")),
        check_vma=False,
    )
```

```python
import functools

import jax
import jax.numpy as jnp
from jax import lax
from jax.experimental import pallas as pl
from jax.experimental.pallas import tpu as pltpu
from jax.sharding import PartitionSpec as P

EXPERTS = 4
TOP = 2
CAP = 12
LANES = 128
VMEM_LIMIT = 6 << 20
LOADS = 4
F32 = jnp.float32
BF16 = jnp.bfloat16
NT = (((1,), (1,)), ((), ()))
IN_VMEM = pl.BlockSpec(memory_space=pltpu.VMEM)
IN_SMEM = pl.BlockSpec(memory_space=pltpu.SMEM)
IN_HBM = pl.BlockSpec(memory_space=pltpu.HBM)
ANYWHERE = pl.BlockSpec(memory_space=pl.ANY)


def swapped(value, axis, by):
    devices = lax.axis_size(axis)
    return lax.ppermute(value, axis, [(i, i ^ by) for i in range(devices)])


def iota(shape, dim):
    return lax.broadcasted_iota(jnp.int32, shape, dim)


def one_hot(mask):
    return mask.astype(F32).astype(BF16)


def token_flip(tokens, by):
    shape = (tokens, tokens)
    return one_hot((iota(shape, 0) ^ by) == iota(shape, 1))


def silu(v):
    return v / (1.0 + jnp.exp(-v))


def mate_of(labels):
    mate = 0
    for i in range(1, EXPERTS):
        mate = mate + jnp.where(labels[i] == labels[0], i, 0)
    return mate


def notes_kernel(ids, codes, *refs):
    notes = refs[-1]
    shard = ids.shape[1]
    shape = (LANES, shard)
    line = iota(shape, 0)
    picked = jnp.zeros(shape, F32)
    scale = jnp.zeros(shape, F32)
    for k in range(TOP):
        own = ids[k:k + 1, :]
        picked = picked + (own == line).astype(F32)
        weight = codes[k:k + 1, :].astype(F32) / 256.0
        scale = scale + jnp.where(own == line - EXPERTS, weight, 0.0)
    square = (shard, shard)
    earlier = (iota(square, 0) < iota(square, 1)).astype(F32)
    same = (iota(square, 0) == iota(square, 1)).astype(F32)
    slot = jnp.dot(picked, earlier, preferred_element_type=F32)
    slot = jnp.where(picked > 0.0, slot, -1.0)
    table = jnp.where(line < EXPERTS, slot, scale)
    notes[...] = lax.dot_general(same, table, NT, preferred_element_type=F32).astype(BF16)


def load_kernel(place, gate_w, up_w, *refs, ks):
    blocks, done, sems = refs[-3:]
    rows = blocks.shape[2] // LOADS
    depth = blocks.shape[3]
    copies = []
    for i, k in enumerate(ks):
        columns = pl.ds(pl.multiple_of((place[0] ^ k) * depth, LANES), depth)
        for w, weight in enumerate((gate_w, up_w)):
            for p in range(LOADS):
                part = pl.ds(p * rows, rows)
                copies.append(
                    pltpu.make_async_copy(
                        weight.at[part, columns], blocks.at[w, k, part], sems.at[w, i, p]
                    )
                )
    for copy in copies:
        copy.start()
    for copy in copies:
        copy.wait()
    done[...] = jnp.zeros(done.shape, F32)


def load_down_kernel(weight, *refs):
    held, done, sems = refs[-3:]
    rows = weight.shape[0] // (4 * LOADS)
    copies = []
    for p in range(4 * LOADS):
        part = pl.ds(p * rows, rows)
        copies.append(pltpu.make_async_copy(weight.at[part], held.at[part], sems.at[p]))
    for copy in copies:
        copy.start()
    for copy in copies:
        copy.wait()
    done[...] = jnp.zeros(done.shape, F32)


def product(place, blocks, x, j, w):
    size = blocks.shape[2] // EXPERTS
    depth = blocks.shape[3]
    rows = pl.ds(pl.multiple_of((place[1] ^ j) * size, 16), size)
    total = None
    for i in range(blocks.shape[1]):
        part = lax.dot_general(
            blocks[w, i, rows], x[:, LANES + i * depth:LANES + (i + 1) * depth], NT, preferred_element_type=F32
        )
        total = part if total is None else total + part
    return total


def picks(notes, expert, rows, shard):
    table = notes.astype(F32).T
    slot = jnp.sum(jnp.where(iota(table.shape, 0) == expert, table, 0.0), axis=0, keepdims=True)
    tokens = slot.shape[1]
    first = (iota((1, tokens), 1) // shard) * CAP
    target = jnp.where(slot < 0.0, -1, first + slot.astype(jnp.int32))
    return one_hot(iota((rows, tokens), 0) == target)


def project_sent_kernel(place, x, blocks, slots, *sent, shard):
    size = blocks.shape[2] // EXPERTS
    pick = picks(x[:, :LANES], place[1], slots.shape[0], shard)
    for j in range(1, EXPERTS):
        gate = product(place, blocks, x, j, 0)
        upper = product(place, blocks, x, j, 1)
        sent[j - 1][0] = gate.astype(BF16)
        sent[j - 1][1] = upper.astype(BF16)
        hidden = (silu(gate) * upper).T.astype(BF16)
        slots[:, (j - 1) * size:j * size] = jnp.dot(
            pick, hidden, preferred_element_type=F32
        ).astype(BF16)


def project_own_kernel(place, x, blocks, others, slots, own, *, shard):
    size = blocks.shape[2] // EXPERTS
    pick = picks(x[:, :LANES], place[1], slots.shape[0], shard)
    gate = product(place, blocks, x, 0, 0)
    upper = product(place, blocks, x, 0, 1)
    own[0] = gate
    own[1] = upper
    hidden = (silu(gate) * upper).T.astype(BF16)
    slots[:, :size] = jnp.dot(pick, hidden, preferred_element_type=F32).astype(BF16)
    slots[:, size:] = others[...]


def merge_kernel(place, labels, freq, own, *refs, flips):
    peers, hidden = refs[:EXPERTS - 1], refs[-1]
    expert = place[1]
    mate = mate_of(labels)
    tokens = own.shape[2]
    parts = [own]
    counts = [jnp.full((1, 1), freq[expert], jnp.int32).astype(F32)]
    for j, peer in enumerate(peers, 1):
        order = token_flip(tokens, flips[j - 1])
        parts.append([jnp.dot(peer[i], order, preferred_element_type=F32) for i in range(2)])
        counts.append(jnp.full((1, 1), freq[expert ^ j], jnp.int32).astype(F32))
    for group in range(2):
        member = []
        for j in range(EXPERTS):
            same = jnp.logical_or(j == 0, mate == j)
            member.append(jnp.where(same if group == 0 else jnp.logical_not(same), counts[j], 0.0))
        whole = member[0] + member[1] + member[2] + member[3]
        gate, upper = [
            sum((member[j] / whole) * parts[j][i] for j in range(EXPERTS)) for i in range(2)
        ]
        hidden[group] = (silu(gate) * upper).T.astype(BF16)


def route_kernel(labels, *refs, count):
    pieces, sent = refs[:count], refs[1 - EXPERTS:]
    mate = mate_of(labels)
    for j, to in enumerate(sent, 1):
        group = jnp.where(mate == j, 0, 1)
        for i in range(count):
            to[i] = pieces[i][group]


def times_weight(place, weight, hidden, ks, n_exp, factor, store):
    z, expert = place[0], place[1]
    depth = weight.shape[0] // n_exp
    size = depth // EXPERTS
    width = weight.shape[1]
    step = min(256, width)
    for n in range(0, width, step):
        total = None
        for i, k in enumerate(ks):
            for j in range(EXPERTS):
                at = pl.multiple_of((z ^ k) * depth + (expert ^ j) * size, 16)
                part = jnp.dot(
                    hidden[:, (i * EXPERTS + j) * size:(i * EXPERTS + j + 1) * size],
                    weight[pl.ds(at, size), n:n + step],
                    preferred_element_type=F32,
                )
                total = part if total is None else total + part
        store(n, step, total * factor)


def first_down_kernel(place, notes, weight, *refs, shard, n_exp):
    pieces, (out, hidden) = refs[:n_exp], refs[-2:]
    expert = place[1]
    depth = weight.shape[0] // n_exp
    table = notes[...].astype(F32)
    tokens = table.shape[0]
    lane = iota(table.shape, 1)
    slot = jnp.sum(jnp.where(lane == expert, table, 0.0), axis=1, keepdims=True)
    factor = jnp.sum(jnp.where(lane == EXPERTS + expert, table, 0.0), axis=1, keepdims=True)
    first = (iota((tokens, 1), 0) // shard) * CAP
    target = jnp.where(slot < 0.0, -1, first + slot.astype(jnp.int32))
    spread = one_hot(iota((tokens, pieces[0].shape[0]), 1) == target)
    for k, piece in enumerate(pieces):
        hidden[:, k * depth:(k + 1) * depth] = jnp.dot(
            spread, piece[...], preferred_element_type=F32
        ).astype(BF16)

    def store(n, step, total):
        out[:, n:n + step] = total

    times_weight(place, weight, hidden, range(n_exp), n_exp, factor, store)


def second_down_kernel(place, labels, freq, notes, weight, initial, *refs, flips, n_exp, shard):
    own, refs = refs[:n_exp], refs[n_exp:]
    peers, (keep, sent, hidden) = refs[:-3], refs[-3:]
    expert = place[1]
    size = weight.shape[0] // n_exp // EXPERTS
    table = notes[...].astype(F32)
    tokens = table.shape[0]
    mate = mate_of(labels)
    lane = iota(table.shape, 1)
    mine = jnp.logical_or(lane == EXPERTS + expert, lane == EXPERTS + (expert ^ mate))
    factor = jnp.sum(jnp.where(mine, table, 0.0), axis=1, keepdims=True)
    chosen = jnp.full((1, 1), freq[expert], jnp.int32).astype(F32)
    other = jnp.full((1, 1), freq[expert ^ mate], jnp.int32).astype(F32)
    factor = factor * (chosen / (chosen + other))
    for j in range(1, EXPERTS):
        order = token_flip(tokens, flips[j - 1])
        found = []
        for part in peers[j - 1::EXPERTS - 1]:
            found += [part[i] for i in range(part.shape[0])]
        for k in range(n_exp):
            at = (k * EXPERTS + j) * size
            hidden[:, at:at + size] = jnp.dot(
                order, found[k], preferred_element_type=F32
            ).astype(BF16)
    for k in range(n_exp):
        hidden[:, k * EXPERTS * size:(k * EXPERTS + 1) * size] = own[k][0]
    middle = tokens // 2

    def put(index, n, step, total):
        for c in range(middle // shard):
            rows = slice(c * shard, (c + 1) * shard)
            keep[c, index, :, n:n + step] = total[rows]
            rows = slice(middle + c * shard, middle + (c + 1) * shard)
            sent[c, index, :, n:n + step] = total[rows].astype(BF16)

    def store(n, step, total):
        put(0, n, step, initial[:, n:n + step])
        put(1, n, step, total)

    times_weight(place, weight, hidden, range(n_exp), n_exp, factor, store)


def cores_kernel(keep, theirs, own, *sent):
    own[...] = keep[0] + theirs[0].astype(F32)
    for c, to in enumerate(sent, 1):
        to[...] = (keep[c] + theirs[c].astype(F32)).astype(BF16)


def finish_kernel(own, *refs):
    parts, outs = refs[:-2], refs[-2:]
    for i, out in enumerate(outs):
        total = own[i]
        for part in parts:
            total = total + part[i].astype(F32)
        out[...] = total.astype(BF16)


def local(tokens, route_ids, gate_codes, merge_labels, freq_counts, w_gate, w_up, w_down):
    n_tok = lax.axis_size("tok")
    n_exp = lax.axis_size("exp")
    span = n_tok // EXPERTS
    z = lax.axis_index("exp")
    expert = lax.axis_index("tok") // span
    shard, depth = tokens.shape
    all_tokens = n_tok * shard
    units = w_gate.shape[0]
    size = units // EXPERTS
    width = w_down.shape[1]
    half = n_exp // 2
    flips = tuple(j * span // 2 * shard for j in range(1, EXPERTS))
    others = range(1, EXPERTS)
    gate_w = pltpu.with_memory_space_constraint(w_gate, pltpu.HBM)
    up_w = pltpu.with_memory_space_constraint(w_up, pltpu.HBM)
    down_w = pltpu.with_memory_space_constraint(w_down, pltpu.HBM)
    place = jnp.stack([z, expert]).astype(jnp.int32)
    shape = jax.ShapeDtypeStruct

    small = pl.CostEstimate(flops=1, bytes_accessed=1, transcendentals=0)
    limit = VMEM_LIMIT if all_tokens <= LANES else 2 * VMEM_LIMIT

    def call(kernel, name, out_shape, *args, scratch=(), smem=0, unused=0, hbm=0, cost=True):
        specs = [IN_SMEM] * smem + [IN_HBM] * hbm
        specs += [IN_VMEM] * (len(args) - len(specs) - unused) + [ANYWHERE] * unused
        return pl.pallas_call(
            kernel,
            in_specs=specs,
            out_specs=[IN_VMEM] * len(out_shape) if isinstance(out_shape, list) else IN_VMEM,
            out_shape=out_shape,
            scratch_shapes=scratch,
            compiler_params=pltpu.CompilerParams(vmem_limit_bytes=limit),
            cost_estimate=small if cost else None,
            name=name,
        )(*args)

    def load(ks, before=None, *after):
        aliased = [] if before is None else [before]
        blocks = (2, n_exp, units, depth)
        return pl.pallas_call(
            functools.partial(load_kernel, ks=ks),
            in_specs=[IN_SMEM, IN_HBM, IN_HBM]
            + [IN_VMEM] * len(aliased)
            + [ANYWHERE] * len(after),
            out_specs=[IN_VMEM] * 2,
            out_shape=[pltpu.VMEM(blocks, BF16), shape((8, LANES), F32)],
            scratch_shapes=[pltpu.SemaphoreType.DMA((2, len(ks), LOADS))],
            input_output_aliases={3: 0} if aliased else {},
            compiler_params=pltpu.CompilerParams(vmem_limit_bytes=limit),
            name="load",
        )(place, gate_w, up_w, *aliased, *after)

    weights, done = load(range(half))
    notes = call(
        notes_kernel,
        "notes",
        shape((shard, LANES), BF16),
        route_ids.T,
        gate_codes.T,
        done,
        unused=1,
    )
    with jax.named_scope("gather_tokens"):
        row = jnp.concatenate(
            [notes, tokens] + [swapped(tokens, "exp", k) for k in range(1, n_exp)], axis=1
        )
        weights, _ = load(range(half, n_exp), weights, row)
        chips = jnp.concatenate(
            [row] + [swapped(row, "tok", j) for j in range(2, n_tok, 2)], axis=0
        )
        x = jnp.concatenate([chips, swapped(chips, "tok", 1)], axis=0)
        table = x[:, :LANES]

    others_slots, *sent = call(
        functools.partial(project_sent_kernel, shard=shard),
        "project_sent",
        [shape((n_tok * CAP, units - size), BF16)]
        + [shape((2, size, all_tokens), BF16) for _ in others],
        place,
        x,
        weights,
        smem=1,
        cost=False,
    )
    with jax.named_scope("peers"):
        peers = [swapped(sent[j - 1], "tok", j * span) for j in others]
    slots, own = call(
        functools.partial(project_own_kernel, shard=shard),
        "project_own",
        [shape((n_tok * CAP, units), BF16), shape((2, size, all_tokens), F32)],
        place,
        x,
        weights,
        others_slots,
        smem=1,
        cost=False,
    )
    early = n_exp // 2
    with jax.named_scope("spread_first"):
        sooner = swapped(slots, "exp", early)
    down_v, down_done = call(
        load_down_kernel,
        "load_down",
        [pltpu.VMEM(w_down.shape, BF16), shape((8, LANES), F32)],
        down_w,
        slots,
        scratch=[pltpu.SemaphoreType.DMA((4 * LOADS,))],
        hbm=1,
        unused=1,
        cost=False,
    )
    merged = call(
        functools.partial(merge_kernel, flips=flips),
        "merge",
        shape((2, all_tokens, size), BF16),
        place,
        merge_labels,
        freq_counts,
        own,
        *peers,
        sooner,
        down_done,
        smem=3,
        unused=2,
    )
    with jax.named_scope("spread_second"):
        second = [merged] + [swapped(merged, "exp", k) for k in range(1, n_exp)]
    def grouped(pieces, *after):
        out = call(
            functools.partial(route_kernel, count=len(pieces)),
            "route",
            [shape((len(pieces), all_tokens, size), BF16) for _ in others],
            merge_labels,
            *pieces,
            *after,
            smem=1,
            unused=len(after),
        )
        with jax.named_scope("groups"):
            return out, [swapped(out[j - 1], "tok", j * span) for j in others]

    own_out, groups = grouped(second[:n_exp // 2])
    beside, _ = lax.optimization_barrier((slots, own_out[0]))
    waiting, *_ = lax.optimization_barrier((slots, second[n_exp // 2]))
    with jax.named_scope("spread_first"):
        first = [slots]
        for k in range(1, n_exp):
            if k == n_exp // 2:
                first.append(sooner)
            elif k < n_exp // 2:
                first.append(swapped(beside, "exp", k))
            else:
                first.append(swapped(waiting, "exp", k))
    far_out, more = grouped(second[n_exp // 2:], *groups)
    initial = call(
        functools.partial(first_down_kernel, shard=shard, n_exp=n_exp),
        "first_down",
        shape((all_tokens, width), F32),
        place,
        table,
        down_v,
        *first,
        far_out[0],
        scratch=[pltpu.VMEM((all_tokens, n_exp * units), BF16)],
        smem=1,
        unused=1,
        cost=False,
    )
    ends = (n_tok // 2, 2, shard, width)
    keep, sent = call(
        functools.partial(second_down_kernel, flips=flips, n_exp=n_exp, shard=shard),
        "second_down",
        [shape(ends, F32), shape(ends, BF16)],
        place,
        merge_labels,
        freq_counts,
        table,
        down_v,
        initial,
        *second,
        *groups,
        *more,
        scratch=[pltpu.VMEM((all_tokens, n_exp * units), BF16)],
        smem=3,
        cost=False,
    )
    with jax.named_scope("cores"):
        theirs = swapped(sent, "tok", 1)
    piece = (2, shard, width)
    own, *sent = call(
        cores_kernel,
        "cores",
        [shape(piece, F32)] + [shape(piece, BF16) for _ in range(1, n_tok // 2)],
        keep,
        theirs,
    )
    with jax.named_scope("chips"):
        parts = [swapped(value, "tok", 2 * c) for c, value in enumerate(sent, 1)]
    return tuple(
        call(finish_kernel, "finish", [shape((shard, width), BF16)] * 2, own, *parts)
    )


def solution(mesh):
    return jax.shard_map(
        local,
        mesh=mesh,
        in_specs=(
            P("tok", "exp"),
            P("tok", None),
            P("tok", None),
            P(),
            P(),
            P(("tok", "exp"), None),
            P(("tok", "exp"), None),
            P("tok", "exp"),
        ),
        out_specs=(P("tok", "exp"), P("tok", "exp")),
        check_vma=False,
    )
```

```python
import functools

import jax
import jax.numpy as jnp
from jax import lax
from jax.experimental import pallas as pl
from jax.experimental.pallas import tpu as pltpu
from jax.sharding import PartitionSpec as P

EXPERTS = 4
TOP = 2
CAP = 12
LANES = 128
VMEM_LIMIT = 6 << 20
LOADS = 4
F32 = jnp.float32
BF16 = jnp.bfloat16
NT = (((1,), (1,)), ((), ()))
IN_VMEM = pl.BlockSpec(memory_space=pltpu.VMEM)
IN_SMEM = pl.BlockSpec(memory_space=pltpu.SMEM)
IN_HBM = pl.BlockSpec(memory_space=pltpu.HBM)
ANYWHERE = pl.BlockSpec(memory_space=pl.ANY)


def swapped(value, axis, by):
    devices = lax.axis_size(axis)
    return lax.ppermute(value, axis, [(i, i ^ by) for i in range(devices)])


def iota(shape, dim):
    return lax.broadcasted_iota(jnp.int32, shape, dim)


def one_hot(mask):
    return mask.astype(F32).astype(BF16)


def token_flip(tokens, by):
    shape = (tokens, tokens)
    return one_hot((iota(shape, 0) ^ by) == iota(shape, 1))


def silu(v):
    return v / (1.0 + jnp.exp(-v))


def mate_of(labels):
    mate = 0
    for i in range(1, EXPERTS):
        mate = mate + jnp.where(labels[i] == labels[0], i, 0)
    return mate


def notes_kernel(ids, codes, *refs):
    notes = refs[-1]
    shard = ids.shape[1]
    shape = (LANES, shard)
    line = iota(shape, 0)
    picked = jnp.zeros(shape, F32)
    scale = jnp.zeros(shape, F32)
    for k in range(TOP):
        own = ids[k:k + 1, :]
        picked = picked + (own == line).astype(F32)
        weight = codes[k:k + 1, :].astype(F32) / 256.0
        scale = scale + jnp.where(own == line - EXPERTS, weight, 0.0)
    square = (shard, shard)
    earlier = (iota(square, 0) < iota(square, 1)).astype(F32)
    same = (iota(square, 0) == iota(square, 1)).astype(F32)
    slot = jnp.dot(picked, earlier, preferred_element_type=F32)
    slot = jnp.where(picked > 0.0, slot, -1.0)
    table = jnp.where(line < EXPERTS, slot, scale)
    notes[...] = lax.dot_general(same, table, NT, preferred_element_type=F32).astype(BF16)


def load_kernel(place, gate_w, up_w, *refs, ks):
    blocks, done, sems = refs[-3:]
    rows = blocks.shape[2] // LOADS
    depth = blocks.shape[3]
    copies = []
    for i, k in enumerate(ks):
        columns = pl.ds(pl.multiple_of((place[0] ^ k) * depth, LANES), depth)
        for w, weight in enumerate((gate_w, up_w)):
            for p in range(LOADS):
                part = pl.ds(p * rows, rows)
                copies.append(
                    pltpu.make_async_copy(
                        weight.at[part, columns], blocks.at[w, k, part], sems.at[w, i, p]
                    )
                )
    for copy in copies:
        copy.start()
    for copy in copies:
        copy.wait()
    done[...] = jnp.zeros(done.shape, F32)


def load_down_kernel(weight, *refs):
    held, done, sems = refs[-3:]
    rows = weight.shape[0] // (4 * LOADS)
    copies = []
    for p in range(4 * LOADS):
        part = pl.ds(p * rows, rows)
        copies.append(pltpu.make_async_copy(weight.at[part], held.at[part], sems.at[p]))
    for copy in copies:
        copy.start()
    for copy in copies:
        copy.wait()
    done[...] = jnp.zeros(done.shape, F32)


def product(place, blocks, x, j, w):
    size = blocks.shape[2] // EXPERTS
    depth = blocks.shape[3]
    rows = pl.ds(pl.multiple_of((place[1] ^ j) * size, 16), size)
    total = None
    for i in range(blocks.shape[1]):
        part = lax.dot_general(
            blocks[w, i, rows], x[:, LANES + i * depth:LANES + (i + 1) * depth], NT, preferred_element_type=F32
        )
        total = part if total is None else total + part
    return total


def picks(notes, expert, rows, shard):
    table = notes.astype(F32).T
    slot = jnp.sum(jnp.where(iota(table.shape, 0) == expert, table, 0.0), axis=0, keepdims=True)
    tokens = slot.shape[1]
    first = (iota((1, tokens), 1) // shard) * CAP
    target = jnp.where(slot < 0.0, -1, first + slot.astype(jnp.int32))
    return one_hot(iota((rows, tokens), 0) == target)


def project_sent_kernel(place, x, blocks, slots, *sent, shard):
    size = blocks.shape[2] // EXPERTS
    pick = picks(x[:, :LANES], place[1], slots.shape[0], shard)
    for j in range(1, EXPERTS):
        gate = product(place, blocks, x, j, 0)
        upper = product(place, blocks, x, j, 1)
        sent[j - 1][0] = gate.astype(BF16)
        sent[j - 1][1] = upper.astype(BF16)
        hidden = (silu(gate) * upper).T.astype(BF16)
        slots[:, (j - 1) * size:j * size] = jnp.dot(
            pick, hidden, preferred_element_type=F32
        ).astype(BF16)


def project_own_kernel(place, x, blocks, others, slots, own, *, shard):
    size = blocks.shape[2] // EXPERTS
    pick = picks(x[:, :LANES], place[1], slots.shape[0], shard)
    gate = product(place, blocks, x, 0, 0)
    upper = product(place, blocks, x, 0, 1)
    own[0] = gate
    own[1] = upper
    hidden = (silu(gate) * upper).T.astype(BF16)
    slots[:, :size] = jnp.dot(pick, hidden, preferred_element_type=F32).astype(BF16)
    slots[:, size:] = others[...]


def merge_kernel(place, labels, freq, own, *refs, flips):
    peers, hidden = refs[:EXPERTS - 1], refs[-1]
    expert = place[1]
    mate = mate_of(labels)
    tokens = own.shape[2]
    parts = [own]
    counts = [jnp.full((1, 1), freq[expert], jnp.int32).astype(F32)]
    for j, peer in enumerate(peers, 1):
        order = token_flip(tokens, flips[j - 1])
        parts.append([jnp.dot(peer[i], order, preferred_element_type=F32) for i in range(2)])
        counts.append(jnp.full((1, 1), freq[expert ^ j], jnp.int32).astype(F32))
    for group in range(2):
        member = []
        for j in range(EXPERTS):
            same = jnp.logical_or(j == 0, mate == j)
            member.append(jnp.where(same if group == 0 else jnp.logical_not(same), counts[j], 0.0))
        whole = member[0] + member[1] + member[2] + member[3]
        gate, upper = [
            sum((member[j] / whole) * parts[j][i] for j in range(EXPERTS)) for i in range(2)
        ]
        hidden[group] = (silu(gate) * upper).T.astype(BF16)


def route_kernel(labels, *refs, count):
    pieces, sent = refs[:count], refs[1 - EXPERTS:]
    mate = mate_of(labels)
    for j, to in enumerate(sent, 1):
        group = jnp.where(mate == j, 0, 1)
        for i in range(count):
            to[i] = pieces[i][group]


def times_weight(place, weight, hidden, ks, n_exp, factor, store):
    z, expert = place[0], place[1]
    depth = weight.shape[0] // n_exp
    size = depth // EXPERTS
    width = weight.shape[1]
    step = min(256, width)
    for n in range(0, width, step):
        total = None
        for i, k in enumerate(ks):
            for j in range(EXPERTS):
                at = pl.multiple_of((z ^ k) * depth + (expert ^ j) * size, 16)
                part = jnp.dot(
                    hidden[:, (i * EXPERTS + j) * size:(i * EXPERTS + j + 1) * size],
                    weight[pl.ds(at, size), n:n + step],
                    preferred_element_type=F32,
                )
                total = part if total is None else total + part
        store(n, step, total * factor)


def first_down_kernel(place, notes, weight, *refs, shard, n_exp):
    pieces, (out, hidden) = refs[:n_exp], refs[-2:]
    expert = place[1]
    depth = weight.shape[0] // n_exp
    table = notes[...].astype(F32)
    tokens = table.shape[0]
    lane = iota(table.shape, 1)
    slot = jnp.sum(jnp.where(lane == expert, table, 0.0), axis=1, keepdims=True)
    factor = jnp.sum(jnp.where(lane == EXPERTS + expert, table, 0.0), axis=1, keepdims=True)
    first = (iota((tokens, 1), 0) // shard) * CAP
    target = jnp.where(slot < 0.0, -1, first + slot.astype(jnp.int32))
    spread = one_hot(iota((tokens, pieces[0].shape[0]), 1) == target)
    for k, piece in enumerate(pieces):
        hidden[:, k * depth:(k + 1) * depth] = jnp.dot(
            spread, piece[...], preferred_element_type=F32
        ).astype(BF16)

    def store(n, step, total):
        out[:, n:n + step] = total

    times_weight(place, weight, hidden, range(n_exp), n_exp, factor, store)


def second_down_kernel(place, labels, freq, notes, weight, initial, *refs, flips, n_exp, shard):
    own, refs = refs[:n_exp], refs[n_exp:]
    peers, (keep, sent, hidden) = refs[:-3], refs[-3:]
    expert = place[1]
    size = weight.shape[0] // n_exp // EXPERTS
    table = notes[...].astype(F32)
    tokens = table.shape[0]
    mate = mate_of(labels)
    lane = iota(table.shape, 1)
    mine = jnp.logical_or(lane == EXPERTS + expert, lane == EXPERTS + (expert ^ mate))
    factor = jnp.sum(jnp.where(mine, table, 0.0), axis=1, keepdims=True)
    chosen = jnp.full((1, 1), freq[expert], jnp.int32).astype(F32)
    other = jnp.full((1, 1), freq[expert ^ mate], jnp.int32).astype(F32)
    factor = factor * (chosen / (chosen + other))
    for j in range(1, EXPERTS):
        order = token_flip(tokens, flips[j - 1])
        found = []
        for part in peers[j - 1::EXPERTS - 1]:
            found += [part[i] for i in range(part.shape[0])]
        for k in range(n_exp):
            at = (k * EXPERTS + j) * size
            hidden[:, at:at + size] = jnp.dot(
                order, found[k], preferred_element_type=F32
            ).astype(BF16)
    for k in range(n_exp):
        hidden[:, k * EXPERTS * size:(k * EXPERTS + 1) * size] = own[k][0]
    middle = tokens // 2

    def put(index, n, step, total):
        for c in range(middle // shard):
            rows = slice(c * shard, (c + 1) * shard)
            keep[c, index, :, n:n + step] = total[rows]
            rows = slice(middle + c * shard, middle + (c + 1) * shard)
            sent[c, index, :, n:n + step] = total[rows].astype(BF16)

    def store(n, step, total):
        put(0, n, step, initial[:, n:n + step])
        put(1, n, step, total)

    times_weight(place, weight, hidden, range(n_exp), n_exp, factor, store)


def cores_kernel(keep, theirs, own, *sent):
    own[...] = keep[0] + theirs[0].astype(F32)
    for c, to in enumerate(sent, 1):
        to[...] = (keep[c] + theirs[c].astype(F32)).astype(BF16)


def finish_kernel(own, *refs):
    parts, outs = refs[:-2], refs[-2:]
    for i, out in enumerate(outs):
        total = own[i]
        for part in parts:
            total = total + part[i].astype(F32)
        out[...] = total.astype(BF16)


def local(tokens, route_ids, gate_codes, merge_labels, freq_counts, w_gate, w_up, w_down):
    n_tok = lax.axis_size("tok")
    n_exp = lax.axis_size("exp")
    span = n_tok // EXPERTS
    z = lax.axis_index("exp")
    expert = lax.axis_index("tok") // span
    shard, depth = tokens.shape
    all_tokens = n_tok * shard
    units = w_gate.shape[0]
    size = units // EXPERTS
    width = w_down.shape[1]
    half = n_exp // 2
    flips = tuple(j * span // 2 * shard for j in range(1, EXPERTS))
    others = range(1, EXPERTS)
    gate_w = pltpu.with_memory_space_constraint(w_gate, pltpu.HBM)
    up_w = pltpu.with_memory_space_constraint(w_up, pltpu.HBM)
    down_w = pltpu.with_memory_space_constraint(w_down, pltpu.HBM)
    place = jnp.stack([z, expert]).astype(jnp.int32)
    shape = jax.ShapeDtypeStruct

    small = pl.CostEstimate(flops=1, bytes_accessed=1, transcendentals=0)
    limit = VMEM_LIMIT if all_tokens <= LANES else 2 * VMEM_LIMIT

    def call(kernel, name, out_shape, *args, scratch=(), smem=0, unused=0, hbm=0, cost=True):
        specs = [IN_SMEM] * smem + [IN_HBM] * hbm
        specs += [IN_VMEM] * (len(args) - len(specs) - unused) + [ANYWHERE] * unused
        return pl.pallas_call(
            kernel,
            in_specs=specs,
            out_specs=[IN_VMEM] * len(out_shape) if isinstance(out_shape, list) else IN_VMEM,
            out_shape=out_shape,
            scratch_shapes=scratch,
            compiler_params=pltpu.CompilerParams(vmem_limit_bytes=limit),
            cost_estimate=small if cost else None,
            name=name,
        )(*args)

    def load(ks, before=None, *after):
        aliased = [] if before is None else [before]
        blocks = (2, n_exp, units, depth)
        return pl.pallas_call(
            functools.partial(load_kernel, ks=ks),
            in_specs=[IN_SMEM, IN_HBM, IN_HBM]
            + [IN_VMEM] * len(aliased)
            + [ANYWHERE] * len(after),
            out_specs=[IN_VMEM] * 2,
            out_shape=[pltpu.VMEM(blocks, BF16), shape((8, LANES), F32)],
            scratch_shapes=[pltpu.SemaphoreType.DMA((2, len(ks), LOADS))],
            input_output_aliases={3: 0} if aliased else {},
            compiler_params=pltpu.CompilerParams(vmem_limit_bytes=limit),
            name="load",
        )(place, gate_w, up_w, *aliased, *after)

    weights, done = load(range(half))
    notes = call(
        notes_kernel,
        "notes",
        shape((shard, LANES), BF16),
        route_ids.T,
        gate_codes.T,
        done,
        unused=1,
    )
    with jax.named_scope("gather_tokens"):
        row = jnp.concatenate(
            [notes, tokens] + [swapped(tokens, "exp", k) for k in range(1, n_exp)], axis=1
        )
        weights, _ = load(range(half, n_exp), weights, row)
        chips = jnp.concatenate(
            [row] + [swapped(row, "tok", j) for j in range(2, n_tok, 2)], axis=0
        )
        x = jnp.concatenate([chips, swapped(chips, "tok", 1)], axis=0)
        table = x[:, :LANES]

    others_slots, *sent = call(
        functools.partial(project_sent_kernel, shard=shard),
        "project_sent",
        [shape((n_tok * CAP, units - size), BF16)]
        + [shape((2, size, all_tokens), BF16) for _ in others],
        place,
        x,
        weights,
        smem=1,
        cost=False,
    )
    with jax.named_scope("peers"):
        peers = [swapped(sent[j - 1], "tok", j * span) for j in others]
    slots, own = call(
        functools.partial(project_own_kernel, shard=shard),
        "project_own",
        [shape((n_tok * CAP, units), BF16), shape((2, size, all_tokens), F32)],
        place,
        x,
        weights,
        others_slots,
        smem=1,
        cost=False,
    )
    early = n_exp // 2
    with jax.named_scope("spread_first"):
        sooner = swapped(slots, "exp", early)
    down_v, down_done = call(
        load_down_kernel,
        "load_down",
        [pltpu.VMEM(w_down.shape, BF16), shape((8, LANES), F32)],
        down_w,
        slots,
        scratch=[pltpu.SemaphoreType.DMA((4 * LOADS,))],
        hbm=1,
        unused=1,
        cost=False,
    )
    merged = call(
        functools.partial(merge_kernel, flips=flips),
        "merge",
        shape((2, all_tokens, size), BF16),
        place,
        merge_labels,
        freq_counts,
        own,
        *peers,
        sooner,
        down_done,
        smem=3,
        unused=2,
    )
    with jax.named_scope("spread_second"):
        second = [merged] + [swapped(merged, "exp", k) for k in range(1, n_exp)]
    def grouped(pieces, *after):
        out = call(
            functools.partial(route_kernel, count=len(pieces)),
            "route",
            [shape((len(pieces), all_tokens, size), BF16) for _ in others],
            merge_labels,
            *pieces,
            *after,
            smem=1,
            unused=len(after),
        )
        with jax.named_scope("groups"):
            return out, [swapped(out[j - 1], "tok", j * span) for j in others]

    own_out, groups = grouped(second[:n_exp // 2])
    beside, _ = lax.optimization_barrier((slots, own_out[0]))
    waiting, *_ = lax.optimization_barrier((slots, second[n_exp // 2]))
    with jax.named_scope("spread_first"):
        first = [slots]
        for k in range(1, n_exp):
            if k == n_exp // 2:
                first.append(sooner)
            elif k < n_exp // 2:
                first.append(swapped(beside, "exp", k))
            else:
                first.append(swapped(waiting, "exp", k))
    far_out, more = grouped(second[n_exp // 2:], first[1], *groups)
    initial = call(
        functools.partial(first_down_kernel, shard=shard, n_exp=n_exp),
        "first_down",
        shape((all_tokens, width), F32),
        place,
        table,
        down_v,
        *first,
        far_out[0],
        scratch=[pltpu.VMEM((all_tokens, n_exp * units), BF16)],
        smem=1,
        unused=1,
        cost=False,
    )
    ends = (n_tok // 2, 2, shard, width)
    keep, sent = call(
        functools.partial(second_down_kernel, flips=flips, n_exp=n_exp, shard=shard),
        "second_down",
        [shape(ends, F32), shape(ends, BF16)],
        place,
        merge_labels,
        freq_counts,
        table,
        down_v,
        initial,
        *second,
        *groups,
        *more,
        scratch=[pltpu.VMEM((all_tokens, n_exp * units), BF16)],
        smem=3,
        cost=False,
    )
    with jax.named_scope("cores"):
        theirs = swapped(sent, "tok", 1)
    piece = (2, shard, width)
    own, *sent = call(
        cores_kernel,
        "cores",
        [shape(piece, F32)] + [shape(piece, BF16) for _ in range(1, n_tok // 2)],
        keep,
        theirs,
    )
    with jax.named_scope("chips"):
        parts = [swapped(value, "tok", 2 * c) for c, value in enumerate(sent, 1)]
    return tuple(
        call(finish_kernel, "finish", [shape((shard, width), BF16)] * 2, own, *parts)
    )


def solution(mesh):
    return jax.shard_map(
        local,
        mesh=mesh,
        in_specs=(
            P("tok", "exp"),
            P("tok", None),
            P("tok", None),
            P(),
            P(),
            P(("tok", "exp"), None),
            P(("tok", "exp"), None),
            P("tok", "exp"),
        ),
        out_specs=(P("tok", "exp"), P("tok", "exp")),
        check_vma=False,
    )
```
